256 devices in a mesh: pool: 128 (over x, z, y), pd: 2 (over core).
Axes of the slice: x: 4, y: 4, z: 8, core: 2. Of those that a mesh axis runs over, the one named last changes fastest.
Arguments:
- q_latent: bfloat16 [8192, 128, 512], P('pool', 'pd')
- q_rope: bfloat16 [8192, 8192], P('pool', 'pd'), may hold values from -6 to 6
- new_latent: bfloat16 [8192, 576], P('pool'), may hold values from -6 to 6
- pool_pages: bfloat16 [2048, 64, 576], P('pool')
- page_owner: int32 [128, 24], P('pool'), may hold values from 0 to 127, as said below
- page_slot: int32 [128, 24], P('pool'), may hold values from 0 to 15, as said below
- prefix_len: int32 [128], P('pool'), may hold values from 1152 to 1536, as said below
- partner: int32 [128], P('pool'), may hold values from 0 to 127, as said below
- dest_slot: int32 [128], P('pool'), may hold values from 0 to 7
- decode_cache: bfloat16 [1024, 64, 576], P('pool'), may hold values from -6 to 6
Outputs:
- context: bfloat16 [8192, 128, 512], P('pool', 'pd')
- decode_out: bfloat16 [1024, 64, 576], P('pool')
The draws below stay inside these ranges and needn't reach their ends.
Inputs may be any that keep to these rules, and one draw needn't show every extreme that they name: `page_owner`: the 24 owners of one stretch are all different; page 0 of every stretch is the same page, at one owner and slot drawn from the seed. `page_slot`: slots within an owner. `prefix_len`: some stretch has the longest prefix. Each decode device is the partner of exactly one stretch; some stretch c and stretch (c + 64) mod 128 are each other's partners.
All inputs are finite; a program needn't handle non-finite values.
Results may differ from the reference program's by a relative error of at most 0.006.
Values may be sent and summed in bfloat16 or wider, within the bound.
No kernel may reach another device: no remote copies, remote signals or barrier semaphores. Data moves between devices by JAX's collectives and lax.ppermute only.
A program may use at most 128 MiB of HBM per device.

```python
import jax
import jax.numpy as jnp
from jax import lax

KVL = 512
ROPE = 64
HEADS = 128
PAGE = 64
CH = 64
SLOTS = 16
DSLOTS = 8
LAT = 576
MAXPG = 24
TOKENS = 8192
N_POOL = 128


def hot_layout(key):
    owner = jax.random.randint(jax.random.fold_in(key, 101), (), 0, N_POOL)
    slot = jax.random.randint(jax.random.fold_in(key, 102), (), 0, SLOTS)
    return (owner, slot)


def hot_rows(key):
    return jax.random.normal(jax.random.fold_in(key, 103), (PAGE, KVL + ROPE), jnp.float32)


def draw_pool_pages(key, part):
    owner, slot = hot_layout(key)
    shared = hot_rows(key)
    key = jax.random.fold_in(key, 3)
    pages = jax.random.normal(key, (N_POOL * SLOTS, PAGE, KVL + ROPE), jnp.float32)
    pages = pages.at[owner * SLOTS + slot].set(shared)
    return pages.astype(jnp.bfloat16)


def draw_q_latent(key, part):
    key = jax.random.fold_in(key, 4)
    values = jax.random.normal(key, (TOKENS, HEADS, KVL), jnp.float32)
    return values.astype(jnp.bfloat16)


def draw_page_owner(key, part):
    owner, slot = hot_layout(key)
    key = jax.random.fold_in(key, 5)
    keys = jax.random.split(key, N_POOL)
    rest = jax.vmap(lambda single: jax.random.permutation(single, N_POOL - 1))(keys)[:, :MAXPG - 1]
    rest = (owner + 1 + rest) % N_POOL
    first = jnp.full((N_POOL, 1), owner, jnp.int32)
    return jnp.concatenate([first, rest.astype(jnp.int32)], axis=1)


def draw_page_slot(key, part):
    owner, slot = hot_layout(key)
    key = jax.random.fold_in(key, 6)
    rest = jax.random.randint(key, (N_POOL, MAXPG - 1), 0, SLOTS)
    first = jnp.full((N_POOL, 1), slot, jnp.int32)
    return jnp.concatenate([first, rest.astype(jnp.int32)], axis=1)


def draw_prefix_len(key, part):
    key = jax.random.fold_in(key, 7)
    lowest = MAXPG * 3 // 4 * PAGE
    lengths = jax.random.randint(key, (N_POOL,), lowest, MAXPG * PAGE + 1)
    longest = jax.random.randint(jax.random.fold_in(key, 1), (), 0, N_POOL)
    return lengths.at[longest].set(MAXPG * PAGE).astype(jnp.int32)


def place_value(order, index, value):
    places = jnp.arange(N_POOL, dtype=jnp.int32)
    where_now = jnp.sum(jnp.where(order == value, places, 0)).astype(jnp.int32)
    current = order[index]
    order = order.at[where_now].set(current)
    return order.at[index].set(value)


def draw_partner(key, part):
    key = jax.random.fold_in(key, 8)
    order = jax.random.permutation(key, N_POOL).astype(jnp.int32)
    first = jax.random.randint(jax.random.fold_in(key, 1), (), 0, N_POOL).astype(jnp.int32)
    second = ((first + N_POOL // 2) % N_POOL).astype(jnp.int32)
    order = place_value(order, first, second)
    order = place_value(order, second, first)
    return order.astype(jnp.int32)


def place_ends(values, rng, low, largest):
    longest = values.shape.index(max(values.shape))
    spots = []
    for shift in (0, 1):
        where = [jax.random.randint(jax.random.fold_in(rng, axis), (), 0, length) for axis, length in enumerate(values.shape)]
        where[longest] = (where[longest] + shift) % values.shape[longest]
        spots.append(tuple(where))
    return values.at[spots[0]].set(low).at[spots[1]].set(largest)


def block_levels(own_key, shape, cuts, least, high):
    factor_of, own = 1.0, jax.random.fold_in(own_key, 6)
    for position, parts in cuts:
        draws = jnp.exp(jax.random.uniform(jax.random.fold_in(own, position), (parts,), jnp.float32, least / len(cuts), high / len(cuts)))
        factor_of = factor_of * jnp.repeat(draws, shape[position] // parts).reshape([-1 if axis == position else 1 for axis in range(len(shape))])
    return factor_of


def normal_values(rng, extent, deviation, limit, cuts=(), held_as=jnp.bfloat16):
    values = jax.random.normal(rng, extent, jnp.float32) * deviation
    if len(cuts) > 0:
        values = block_levels(rng, extent, cuts, -0.22, 0.18) * values
    return jnp.clip(values, min=-limit, max=limit).astype(held_as)


def setup_inputs(seed: int = 0) -> dict:
    splits = jax.random.split(jax.random.key(seed), 11)
    q_latent = draw_q_latent(jax.random.fold_in(splits[10], 71), 0)
    q_rope = normal_values(splits[1], (TOKENS, HEADS * ROPE), 1.0, 6.0, ((0, 128), (1, 2)))
    new_latent = normal_values(splits[2], (TOKENS, LAT), 1.0, 6.0, ((0, 128),))
    pool_pages = draw_pool_pages(jax.random.fold_in(splits[10], 71), 0)
    page_owner = draw_page_owner(jax.random.fold_in(splits[10], 71), 0)
    page_slot = draw_page_slot(jax.random.fold_in(splits[10], 71), 0)
    prefix_len = draw_prefix_len(jax.random.fold_in(splits[10], 71), 0)
    partner = draw_partner(jax.random.fold_in(splits[10], 71), 0)
    dest_slot = place_ends(jax.random.randint(splits[8], (N_POOL,), 0, DSLOTS), jax.random.fold_in(splits[8], 1), 0, DSLOTS - 1).astype(jnp.int32)
    decode_cache = normal_values(splits[9], (N_POOL * DSLOTS, CH, LAT), 1.0, 6.0, ((0, 128),))
    return {"q_latent": q_latent, "q_rope": q_rope, "new_latent": new_latent, "pool_pages": pool_pages, "page_owner": page_owner, "page_slot": page_slot, "prefix_len": prefix_len, "partner": partner, "dest_slot": dest_slot, "decode_cache": decode_cache}


score_scale = 192.0 ** -0.5


def reference(q_latent, q_rope, new_latent, pool_pages, page_owner, page_slot, prefix_len, partner, dest_slot, decode_cache):
    width = KVL + ROPE
    stored = pool_pages.reshape(N_POOL, SLOTS, PAGE, width)
    queries = jnp.concatenate([q_latent, q_rope.reshape(TOKENS, HEADS, ROPE)], axis=2)
    queries = queries.reshape(N_POOL, CH * HEADS, width)
    fresh = new_latent.reshape(N_POOL, CH, width)
    span = MAXPG * PAGE

    def one_stretch(index):
        owners = page_owner[index].astype(jnp.int32)
        slots = page_slot[index].astype(jnp.int32)
        pages = stored[owners, slots].reshape(span, width)
        keys = jnp.concatenate([pages, fresh[index]], axis=0)
        scores = jnp.dot(queries[index], keys.T, preferred_element_type=jnp.float32) * score_scale
        places = jnp.arange(span + CH, dtype=jnp.int32)
        token_of = jnp.arange(CH * HEADS, dtype=jnp.int32) // HEADS
        visible = jnp.where(places[None, :] < span, (places < prefix_len[index])[None, :], (places[None, :] - span) <= token_of[:, None])
        masked = jnp.where(visible, scores, jnp.float32(-1e30))
        top = jnp.max(masked, axis=1)
        weight = jnp.where(visible, jnp.exp(scores - top[:, None]), jnp.float32(0.0))
        total = jnp.sum(weight, axis=1)
        values = jnp.dot(weight.astype(jnp.bfloat16), keys[:, :KVL], preferred_element_type=jnp.float32)
        return (values / total[:, None]).astype(jnp.bfloat16)

    context = lax.map(one_stretch, jnp.arange(N_POOL, dtype=jnp.int32))
    context = context.reshape(TOKENS, HEADS, KVL)
    source = jnp.zeros((N_POOL,), jnp.int32).at[partner.astype(jnp.int32)].set(jnp.arange(N_POOL, dtype=jnp.int32))
    arrived = fresh[source]
    blocks = decode_cache.reshape(N_POOL, DSLOTS, CH, width)
    chosen = jnp.arange(DSLOTS, dtype=jnp.int32)[None, :] == dest_slot.astype(jnp.int32)[:, None]
    updated = jnp.where(chosen[:, :, None, None], arrived[:, None], blocks)
    return context, updated.reshape(N_POOL * DSLOTS, CH, width)
```

```python
import functools

import jax
import jax.numpy as jnp
from jax import lax
from jax.experimental import pallas as pl
from jax.experimental.pallas import tpu as pltpu
from jax.sharding import PartitionSpec as P

score_scale = 192.0 ** (-0.5)
log2_e = 1.4426950408889634
hidden = -1e30
lanes = 128
f32 = jnp.float32
bf16 = jnp.bfloat16


def iota(shape, axis):
    return lax.broadcasted_iota(jnp.int32, shape, axis)


def picks(condition):
    return jnp.where(condition, jnp.float32(1.0), jnp.float32(0.0)).astype(bf16)


def mm(a, b):
    return lax.dot_general(a, b, (((1,), (0,)), ((), ())), preferred_element_type=f32)


def mm_first(a, b):
    return lax.dot_general(a, b, (((0,), (0,)), ((), ())), preferred_element_type=f32)


def mm_last(a, b):
    return lax.dot_general(a, b, (((1,), (1,)), ((), ())), preferred_element_type=f32)


def spread_kernel(half_ref, pages_ref, new_ref, meta_ref, out_ref):
    slots, rows, width = pages_ref.shape
    held = 24
    pages = pages_ref[...].reshape(slots * rows, width)
    fresh = new_ref[...]
    latent = 4 * lanes
    total = rows * held
    out_row = iota((total, 1), 0)
    out_r = out_row // held
    out_k = out_row % held
    in_row = iota((total, slots * rows), 1)
    in_r = in_row % rows
    in_s = in_row // rows
    same = in_r == out_r
    take_latent = picks(same & (in_s == out_k))
    take_rope = picks(same & (in_s // 8 == out_k - 17))
    new_same = iota((total, rows), 1) == out_r
    take_new = picks(new_same & (out_k == 16))
    take_new_rope = picks(new_same & (out_k == 19))
    src = iota((64, latent), 0)
    dst = iota((64, latent), 1)
    tile = picks((src // 16 == dst // lanes) & (src % 16 == dst % 16))
    group = (iota((slots * rows, latent), 1) % lanes) // 16
    slot = iota((slots * rows, latent), 0) // rows
    rope = mm(pages[:, latent:], tile)
    rope = jnp.where(group == slot % 8, rope, 0.0).astype(bf16)
    new_rope = mm(fresh[:, latent:], tile).astype(bf16)
    result = mm(take_latent, pages[:, :latent]) + mm(take_rope, rope)
    result += mm(take_new, fresh[:, :latent]) + mm(take_new_rope, new_rope)
    meta = meta_ref[...].astype(f32)
    for quarter in range(4):
        part = result[:, quarter * lanes : (quarter + 1) * lanes]
        part = jnp.where(out_k == 20, meta, part)
        out_ref[quarter * rows : (quarter + 1) * rows] = part.reshape(rows, held, lanes).astype(bf16)


def spread(half, pages, fresh, meta):
    slots, page, width = pages.shape
    rows = page // 2
    return pl.pallas_call(
        spread_kernel,
        grid_spec=pltpu.PrefetchScalarGridSpec(
            num_scalar_prefetch=1,
            grid=(1,),
            in_specs=[
                pl.BlockSpec((slots, rows, width), lambda i, half: (0, half[0], 0)),
                pl.BlockSpec((rows, width), lambda i, half: (half[0], 0)),
                pl.BlockSpec((1, lanes), lambda i, half: (0, 0)),
            ],
            out_specs=pl.BlockSpec((4 * rows, 24, lanes), lambda i, half: (0, 0, 0)),
        ),
        out_shape=jax.ShapeDtypeStruct((4 * rows, 24, lanes), bf16),
        compiler_params=pltpu.CompilerParams(vmem_limit_bytes=40 * 1024 * 1024),
        cost_estimate=pl.CostEstimate(flops=10**9, bytes_accessed=1_500_000, transcendentals=0),
    )(half, pages, fresh, meta)


def collect_kernel(block, all_ref, mine_ref, out_ref, table_ref):
    step = pl.program_id(0)
    owners = all_ref.shape[0]
    pages = 24

    @pl.when(step == 0)
    def build():
        src = iota((lanes, lanes), 0)
        dst = iota((lanes, lanes), 1)
        tile = picks(src % 16 == dst % 16)
        group = iota((8, lanes), 1) // 16 == iota((8, lanes), 0)
        chunk = 32
        for first in range(0, owners, chunk):
            held = all_ref[first : first + chunk].astype(f32)
            table_ref[first * 16 : (first + chunk) * 16, :lanes] = (
                held[:, :16].reshape(chunk * 16, lanes).astype(bf16)
            )
            pieces = [
                jnp.where(group[None], held[:, 17 + k : 18 + k], 0.0) for k in range(2)
            ]
            rope = jnp.concatenate(pieces, axis=1).reshape(chunk * 16, lanes).astype(bf16)
            table_ref[first * 16 : (first + chunk) * 16, lanes:] = mm(rope, tile).astype(bf16)

    rows = block * pages
    row = iota((rows, 1), 0)
    stretch = row // pages
    place = row % pages
    meta = mine_ref[:, 16:24].astype(f32)[:, 4, :].astype(bf16)
    expand = picks(iota((rows, block), 1) == stretch)
    spread_meta = mm(expand, meta)
    lane = iota((rows, lanes), 1)
    weight = jnp.where(lane == place, 16.0, jnp.where(lane == place + 32, 1.0, 0.0))
    index = jnp.sum(spread_meta * weight, axis=1, keepdims=True).astype(jnp.int32)
    wanted = picks(iota((rows, owners * 16), 1) == index)
    found = mm(wanted, table_ref[...])
    latent = found[:, :lanes].reshape(block, pages, lanes)
    rope = jnp.where(lane // 16 == place % 8, found[:, lanes:], 0.0).astype(bf16)
    last = iota((block * 8, rows), 0)
    other = iota((block * 8, rows), 1)
    gather_rope = picks(
        (last // 8 == other // pages) & (last % 8 - 1 == (other % pages) // 8)
    )
    tail = mm(gather_rope, rope)
    held = all_ref[:, 16:24].astype(f32)
    partner = held[:, 4, 64:65].astype(jnp.int32)
    target = iota((owners, block * 8), 1)
    arrives = partner == target // 8 + step * block
    tail += mm_first(picks(arrives & (target % 8 == 0)), held[:, 0, :].astype(bf16))
    tail += mm_first(picks(arrives & (target % 8 == 4)), held[:, 3, :].astype(bf16))
    tail = tail.reshape(block, 8, lanes)
    out_ref[...] = jnp.concatenate([latent, tail], axis=1).astype(bf16)


def collect(held):
    owners = held.shape[0]
    block = 16
    return pl.pallas_call(
        functools.partial(collect_kernel, block),
        grid=(owners // block,),
        in_specs=[
            pl.BlockSpec(held.shape, lambda i: (0, 0, 0)),
            pl.BlockSpec((block, 24, lanes), lambda i: (i, 0, 0)),
        ],
        out_specs=pl.BlockSpec((block, 32, lanes), lambda i: (i, 0, 0)),
        out_shape=jax.ShapeDtypeStruct((owners, 32, lanes), bf16),
        scratch_shapes=[pltpu.VMEM((owners * 16, 2 * lanes), bf16)],
        compiler_params=pltpu.CompilerParams(vmem_limit_bytes=40 * 1024 * 1024),
        cost_estimate=pl.CostEstimate(flops=4 * 10**9, bytes_accessed=2_000_000, transcendentals=0),
    )(held, held)


def attend_kernel(sub, q_ref, own_ref, peer_ref, new_ref, bias_ref, out_ref, value_ref, key_ref, score_ref):
    latent = 4 * lanes
    rows = own_ref.shape[0] // 4
    pages = 24
    half = rows * pages
    prefix = 2 * half

    @pl.when(pl.program_id(0) == 0)
    def build():
        src = iota((64, lanes), 1)
        dst = iota((64, lanes), 0)
        group = iota((8, lanes), 1) // 16 == iota((8, lanes), 0)
        for side, ref in enumerate((own_ref, peer_ref)):
            at = side * half
            rope_keys = jnp.zeros((64, half), f32)
            for quarter in range(4):
                block = ref[quarter * rows : (quarter + 1) * rows].astype(f32)
                part = block[:, :pages].reshape(half, lanes)
                value_ref[at : at + half, quarter * lanes : (quarter + 1) * lanes] = part.astype(bf16)
                key_ref[quarter * lanes : (quarter + 1) * lanes, at : at + half] = part.T.astype(bf16)
                pieces = [
                    jnp.where(group[None], block[:, 25 + k : 26 + k], 0.0) for k in range(3)
                ]
                rope = jnp.concatenate(pieces, axis=1).reshape(half, lanes).astype(bf16)
                place = picks((dst // 16 == quarter) & (dst % 16 == src % 16))
                rope_keys += mm_last(place, rope)
            key_ref[latent : latent + 64, at : at + half] = rope_keys.astype(bf16)
        fresh = new_ref[...].astype(f32)
        blank = jnp.zeros((64, latent), f32)
        part = jnp.concatenate([fresh[:, :latent], blank], axis=0)
        value_ref[prefix:, :] = part.astype(bf16)
        key_ref[:latent, prefix:] = part.T.astype(bf16)
        rope = jnp.concatenate([fresh[:, latent:], jnp.zeros((64, 64), f32)], axis=0)
        key_ref[latent : latent + 64, prefix:] = rope.T.astype(bf16)
        key_ref[latent + 64 :, :] = bias_ref[...]

    count = q_ref.shape[0] // sub
    factor = jnp.float32(score_scale * log2_e)
    for part in range(count):
        at = slice(part * sub, (part + 1) * sub)
        scores = mm(q_ref[at, :], key_ref[...])
        top = jnp.max(scores, axis=1, keepdims=True)
        weight = jnp.exp2((scores - top) * factor)
        total = jnp.sum(weight, axis=1, keepdims=True)
        summed = mm(weight.astype(bf16), value_ref[...])
        out_ref[at, :] = (summed * (1.0 / total)).astype(bf16)


def attend(queries, own, peer, fresh, bias, block=512, sub=256):
    count, width = queries.shape
    keys = bias.shape[1]
    latent = 4 * lanes
    whole = lambda a: pl.BlockSpec(a.shape, lambda i: (0,) * a.ndim)
    return pl.pallas_call(
        functools.partial(attend_kernel, sub),
        grid=(count // block,),
        in_specs=[
            pl.BlockSpec((block, width), lambda i: (i, 0)),
            whole(own),
            whole(peer),
            whole(fresh),
            whole(bias),
        ],
        out_specs=pl.BlockSpec((block, latent), lambda i: (i, 0)),
        out_shape=jax.ShapeDtypeStruct((count, latent), bf16),
        scratch_shapes=[
            pltpu.VMEM((keys, latent), bf16),
            pltpu.VMEM((width, keys), bf16),
            pltpu.VMEM((8, lanes), f32),
        ],
        compiler_params=pltpu.CompilerParams(vmem_limit_bytes=56 * 1024 * 1024),
        cost_estimate=pl.CostEstimate(
            flops=2 * count * keys * (width + latent), bytes_accessed=11_000_000, transcendentals=count * keys
        ),
    )(queries, own, peer, fresh, bias)


def body(
    q_latent,
    q_rope,
    new_latent,
    pool_pages,
    page_owner,
    page_slot,
    prefix_len,
    partner,
    dest_slot,
    decode_cache,
):
    stretch, heads, latent = q_latent.shape
    rope = q_rope.shape[1] // heads
    slots, page, width = pool_pages.shape
    most = page_owner.shape[1]
    rows = page // 2
    core = lax.axis_index("pd")

    gap = jnp.zeros((1, 8), jnp.int32)
    meta = jnp.concatenate(
        [page_owner, gap, page_slot, gap, partner[:, None], jnp.zeros((1, lanes - 65), jnp.int32)], axis=1
    ).astype(bf16)
    outgoing = spread(core.astype(jnp.int32)[None], pool_pages, new_latent, meta)
    held = lax.all_to_all(outgoing, "pool", split_axis=0, concat_axis=0, tiled=True)

    token = jnp.arange(stretch, dtype=jnp.int32)
    mark = jnp.broadcast_to(
        (token[:, None] == token[None, :]).astype(bf16)[:, None, :], (stretch, heads, stretch)
    )
    queries = jnp.concatenate([q_latent, q_rope.reshape(stretch, heads, rope), mark], axis=2)
    queries = queries.reshape(stretch * heads, latent + rope + stretch)
    key = jnp.arange(rows * most, dtype=jnp.int32)
    spot = (key % most) * page + key // most
    spots = jnp.concatenate([spot + rows * core, spot + rows * (1 - core)])
    seen = jnp.broadcast_to((spots < prefix_len[0])[None, :], (stretch, 2 * rows * most))
    late = jnp.arange(2 * stretch, dtype=jnp.int32)
    causal = late[None, :] <= token[:, None]
    bias = jnp.where(jnp.concatenate([seen, causal], axis=1), 0.0, hidden).astype(bf16)

    replies = collect(held)
    own = lax.all_to_all(replies, "pool", split_axis=0, concat_axis=0, tiled=True)
    peer = lax.ppermute(own, "pd", [(0, 1), (1, 0)])
    context = attend(queries, own, peer, new_latent, bias).reshape(stretch, heads, latent)

    tails = jnp.where(core == 0, jnp.stack([own[:, 24:], peer[:, 24:]]), jnp.stack([peer[:, 24:], own[:, 24:]]))
    tails = tails.reshape(2, 4, rows, 8, lanes)
    first = tails[:, :, :, 0].transpose(0, 2, 1, 3).reshape(page, latent)
    second = tails[:, :, :, 4, :16].transpose(0, 2, 1, 3).reshape(page, rope)
    arrived = jnp.concatenate([first, second], axis=1)
    decode_out = lax.dynamic_update_slice(decode_cache, arrived[None], (dest_slot[0], 0, 0))
    return (context, decode_out)


def solution(mesh):
    placed = (
        P("pool", "pd", None),
        P("pool", "pd"),
        P("pool", None),
        P("pool", None, None),
        P("pool", None),
        P("pool", None),
        P("pool"),
        P("pool"),
        P("pool"),
        P("pool", None, None),
    )
    return jax.shard_map(
        body,
        mesh=mesh,
        in_specs=placed,
        out_specs=(P("pool", "pd", None), P("pool", None, None)),
        check_vma=False,
    )
```

```python
import functools

import jax
import jax.numpy as jnp
from jax import lax
from jax.experimental import pallas as pl
from jax.experimental.pallas import tpu as pltpu
from jax.sharding import PartitionSpec as P

score_scale = 192.0 ** (-0.5)
log2_e = 1.4426950408889634
hidden = -1e30
lanes = 128
f32 = jnp.float32
bf16 = jnp.bfloat16


def iota(shape, axis):
    return lax.broadcasted_iota(jnp.int32, shape, axis)


def picks(condition):
    return jnp.where(condition, jnp.float32(1.0), jnp.float32(0.0)).astype(bf16)


def mm(a, b):
    return lax.dot_general(a, b, (((1,), (0,)), ((), ())), preferred_element_type=f32)


def mm_first(a, b):
    return lax.dot_general(a, b, (((0,), (0,)), ((), ())), preferred_element_type=f32)


def mm_last(a, b):
    return lax.dot_general(a, b, (((1,), (1,)), ((), ())), preferred_element_type=f32)


def spread_kernel(partner_ref, pages_ref, new_ref, owner_ref, slot_ref, out_ref):
    slots = pages_ref.shape[0]
    rows = out_ref.shape[1]
    begin = pl.multiple_of(lax.axis_index("pd") * (2 * rows) + pl.program_id(0) * rows, rows)
    held = 24
    pages = pages_ref[:, pl.ds(begin, rows), :].reshape(slots * rows, pages_ref.shape[2])
    fresh = new_ref[pl.ds(begin, rows), :]
    latent = 4 * lanes
    total = rows * held
    out_row = iota((total, 1), 0)
    out_r = out_row // held
    out_k = out_row % held
    in_row = iota((total, slots * rows), 1)
    in_r = in_row % rows
    in_s = in_row // rows
    same = in_r == out_r
    take_latent = picks(same & (in_s == out_k))
    take_rope = picks(same & (in_s // 8 == out_k - 17))
    new_same = iota((total, rows), 1) == out_r
    take_new = picks(new_same & (out_k == 16))
    take_new_rope = picks(new_same & (out_k == 19))
    src = iota((64, latent), 0)
    dst = iota((64, latent), 1)
    tile = picks((src // 16 == dst // lanes) & (src % 16 == dst % 16))
    group = (iota((slots * rows, latent), 1) % lanes) // 16
    slot = iota((slots * rows, latent), 0) // rows
    rope = mm(pages[:, latent:], tile)
    rope = jnp.where(group == slot % 8, rope, 0.0).astype(bf16)
    new_rope = mm(fresh[:, latent:], tile).astype(bf16)
    result = mm(take_latent, pages[:, :latent]) + mm(take_rope, rope)
    result += mm(take_new, fresh[:, :latent]) + mm(take_new_rope, new_rope)
    asked = owner_ref.shape[1]
    lane = iota((asked, lanes), 1)
    at = iota((asked, lanes), 0)
    meta = mm(owner_ref[...].astype(f32).astype(bf16), picks(lane == at))
    meta += mm(slot_ref[...].astype(f32).astype(bf16), picks(lane == at + 32))
    meta = jnp.where(iota((1, lanes), 1) == 64, partner_ref[0].astype(f32), meta)
    for quarter in range(4):
        part = result[:, quarter * lanes : (quarter + 1) * lanes]
        part = jnp.where(out_k == 20, meta, part)
        out_ref[quarter] = part.reshape(rows, held, lanes).astype(bf16)


def spread(partner, pages, fresh, owner, slot):
    slots, page, width = pages.shape
    rows = page // 4
    whole = lambda a: pl.BlockSpec(a.shape, lambda i: (0,) * a.ndim)
    out = pl.pallas_call(
        spread_kernel,
        grid=(2,),
        in_specs=[
            pl.BlockSpec(memory_space=pltpu.SMEM),
            whole(pages),
            whole(fresh),
            whole(owner),
            whole(slot),
        ],
        out_specs=pl.BlockSpec((4, rows, 24, lanes), lambda i: (0, i, 0, 0)),
        out_shape=jax.ShapeDtypeStruct((4, 2 * rows, 24, lanes), bf16),
        compiler_params=pltpu.CompilerParams(vmem_limit_bytes=60 * 1024 * 1024),
        cost_estimate=pl.CostEstimate(flops=10**9, bytes_accessed=1_500_000, transcendentals=0),
    )(partner, pages, fresh, owner, slot)
    return out.reshape(8 * rows, 24, lanes)


def collect_kernel(pages, group, all_ref, out_ref, rows_ref, table_ref, stage_ref):
    owners, held, _ = all_ref.shape
    slots = 16
    size = 32
    rows_ref[...] = all_ref[...].astype(f32).reshape(owners * held, lanes)
    src = iota((lanes, lanes), 0)
    dst = iota((lanes, lanes), 1)
    tile = picks(src % 16 == dst % 16)
    lane = iota((owners, lanes), 1)
    for slot in range(slots):
        at = slice(slot * owners, (slot + 1) * owners)
        table_ref[at, :lanes] = rows_ref[pl.ds(slot, owners, stride=held), :].astype(bf16)
        piece = rows_ref[pl.ds(17 + slot // 8, owners, stride=held), :]
        piece = jnp.where(lane // 16 == slot % 8, piece, 0.0).astype(bf16)
        table_ref[at, lanes:] = mm(piece, tile).astype(bf16)
    meta = rows_ref[pl.ds(20, owners, stride=held), :]
    blank = jnp.zeros((owners, lanes), f32)
    ropes = [blank] * (pages // 8)
    for start in range(0, pages, group):
        wanted = []
        for place in range(start, start + group):
            owner = picks(meta[:, place : place + 1] == lane.astype(f32))
            slot = jnp.broadcast_to(meta[:, 32 + place : 33 + place], (owners, lanes)).astype(bf16)
            wanted.append(
                jnp.concatenate(
                    [jnp.where(slot == jnp.bfloat16(k), owner, jnp.bfloat16(0)) for k in range(slots)], axis=1
                )
            )
        found = mm(jnp.concatenate(wanted, axis=0), table_ref[...])
        for k in range(group):
            place = start + k
            got = found[k * owners : (k + 1) * owners]
            stage_ref[pl.ds(place, owners, stride=size), :] = got[:, :lanes]
            ropes[place // 8] += jnp.where(lane // 16 == place % 8, got[:, lanes:], 0.0)
    comes = picks(meta[:, 64:65].astype(jnp.int32) == lane)
    arriving = mm_first(comes, rows_ref[pl.ds(16, owners, stride=held), :].astype(bf16))
    arriving_rope = mm_first(comes, rows_ref[pl.ds(19, owners, stride=held), :].astype(bf16))
    tail = [arriving] + ropes + [arriving_rope]
    tail += [blank] * (size - pages - len(tail))
    for k, piece in enumerate(tail):
        stage_ref[pl.ds(pages + k, owners, stride=size), :] = piece
    out_ref[...] = stage_ref[...].reshape(owners, size, lanes).astype(bf16)


def collect(held, pages):
    owners = held.shape[0]
    return pl.pallas_call(
        functools.partial(collect_kernel, pages, 4),
        in_specs=[pl.BlockSpec(memory_space=pltpu.VMEM)],
        out_specs=pl.BlockSpec(memory_space=pltpu.VMEM),
        out_shape=jax.ShapeDtypeStruct((owners, 32, lanes), bf16),
        scratch_shapes=[
            pltpu.VMEM((owners * held.shape[1], lanes), f32),
            pltpu.VMEM((owners * 16, 2 * lanes), bf16),
            pltpu.VMEM((owners * 32, lanes), f32),
        ],
        compiler_params=pltpu.CompilerParams(vmem_limit_bytes=40 * 1024 * 1024),
        cost_estimate=pl.CostEstimate(flops=4 * 10**9, bytes_accessed=1_500_000, transcendentals=0),
    )(held)


factor = score_scale * log2_e


def fresh_kernel(sub, q_ref, new_ref, acc_ref, stat_ref, value_ref, key_ref):
    latent = 4 * lanes

    @pl.when(pl.program_id(0) == 0)
    def build():
        fresh = new_ref[...].astype(f32)
        part = jnp.concatenate([fresh[:, :latent], jnp.zeros((64, latent), f32)], axis=0)
        value_ref[...] = part.astype(bf16)
        key_ref[:latent, :] = part.T.astype(bf16)
        rope = jnp.concatenate([fresh[:, latent:], jnp.zeros((64, 64), f32)], axis=0)
        key_ref[latent : latent + 64, :] = rope.T.astype(bf16)
        token = iota((64, lanes), 0)
        late = iota((64, lanes), 1)
        key_ref[latent + 64 :, :] = jnp.where(late <= token, 0.0, hidden).astype(bf16)

    for part in range(q_ref.shape[0] // sub):
        at = slice(part * sub, (part + 1) * sub)
        scores = mm(q_ref[at, :], key_ref[...])
        top = jnp.max(scores, axis=1, keepdims=True)
        weight = jnp.exp2((scores - top) * jnp.float32(factor))
        total = jnp.sum(weight, axis=1, keepdims=True)
        acc_ref[at, :] = mm(weight.astype(bf16), value_ref[...])
        stat_ref[at, :] = jnp.where(iota((sub, lanes), 1) < 64, top, total)


def attend_fresh(queries, fresh, block=512, sub=256):
    count, width = queries.shape
    latent = 4 * lanes
    return pl.pallas_call(
        functools.partial(fresh_kernel, sub),
        grid=(count // block,),
        in_specs=[
            pl.BlockSpec((block, width), lambda i: (i, 0)),
            pl.BlockSpec(fresh.shape, lambda i: (0, 0)),
        ],
        out_specs=[
            pl.BlockSpec((block, latent), lambda i: (i, 0)),
            pl.BlockSpec((block, lanes), lambda i: (i, 0)),
        ],
        out_shape=[
            jax.ShapeDtypeStruct((count, latent), f32),
            jax.ShapeDtypeStruct((count, lanes), f32),
        ],
        scratch_shapes=[pltpu.VMEM((lanes, latent), bf16), pltpu.VMEM((width, lanes), bf16)],
        compiler_params=pltpu.CompilerParams(vmem_limit_bytes=40 * 1024 * 1024),
        cost_estimate=pl.CostEstimate(flops=5 * 10**9, bytes_accessed=16_000_000, transcendentals=count * lanes),
    )(queries, fresh)


def attend_kernel(
    pages,
    sub,
    chunk,
    length_ref,
    dest_ref,
    q_ref,
    own_ref,
    peer_ref,
    acc_ref,
    stat_ref,
    cache_ref,
    out_ref,
    decode_ref,
    key_ref,
    score_ref,
    arrive_ref,
):
    latent = 4 * lanes
    rows = own_ref.shape[0] // 4
    half = rows * pages
    keys = 2 * half
    step = pl.program_id(0)

    @pl.when(step == 0)
    def build():
        core = lax.axis_index("pd")
        src = iota((lanes, lanes), 0)
        dst = iota((lanes, lanes), 1)
        group = iota((8, lanes), 1) // 16 == iota((8, lanes), 0)
        key = iota((half, 1), 0)
        row = key // pages
        place = (key - row * pages) * 64 + row
        for side, ref in enumerate((own_ref, peer_ref)):
            at = slice(side * half, (side + 1) * half)
            spot = pl.multiple_of((core if side == 0 else 1 - core) * rows, rows)
            rope_keys = jnp.zeros((half, lanes), f32)
            arrived_rope = jnp.zeros((rows, lanes), f32)
            for quarter in range(4):
                cols = slice(quarter * lanes, (quarter + 1) * lanes)
                block = ref[quarter * rows : (quarter + 1) * rows].astype(f32)
                key_ref[at, cols] = block[:, :pages].reshape(half, lanes).astype(bf16)
                tail = block[:, pages:]
                pieces = [jnp.where(group[None], tail[:, 1 + k : 2 + k], 0.0) for k in range(pages // 8)]
                rope = jnp.concatenate(pieces, axis=1).reshape(half, lanes).astype(bf16)
                put = picks((dst // 16 == quarter) & (dst % 16 == src % 16))
                rope_keys += mm(rope, put)
                arrive_ref[pl.ds(spot, rows), cols] = tail[:, 0, :]
                last = jnp.where(iota((rows, lanes), 1) < 16, tail[:, 1 + pages // 8, :], 0.0)
                arrived_rope += mm(last.astype(bf16), put)
            arrive_ref[pl.ds(spot, rows), latent:] = arrived_rope[:, :64]
            bias = jnp.where(place + spot < length_ref[0], 0.0, hidden)
            joined = jnp.where(iota((half, lanes), 1) < 64, rope_keys, bias)
            key_ref[at, latent:] = joined.astype(bf16)

    count = q_ref.shape[0] // sub
    scale = jnp.float32(factor)

    def score(part):
        at = slice(part * sub, (part + 1) * sub)
        top = None
        for begin in range(0, keys, chunk):
            found = mm_last(q_ref[at, :], key_ref[begin : begin + chunk, :])
            score_ref[part % 2, :, begin : begin + chunk] = found
            for k in range(0, chunk, lanes):
                piece = found[:, k : k + lanes]
                top = piece if top is None else jnp.maximum(top, piece)
        return jnp.maximum(jnp.max(top, axis=1, keepdims=True), stat_ref[at, :1])

    def finish(part, top):
        at = slice(part * sub, (part + 1) * sub)
        summed = None
        total = None
        for begin in range(0, keys, chunk):
            weight = jnp.exp2((score_ref[part % 2, :, begin : begin + chunk] - top) * scale)
            for k in range(0, chunk, lanes):
                piece = weight[:, k : k + lanes]
                total = piece if total is None else total + piece
            product = mm(weight.astype(bf16), key_ref[begin : begin + chunk, :latent])
            summed = product if summed is None else summed + product
        shrink = jnp.exp2((stat_ref[at, :1] - top) * scale)
        total = jnp.sum(total, axis=1, keepdims=True) + shrink * stat_ref[at, 64:65]
        summed = summed + shrink * acc_ref[at, :]
        out_ref[at, :] = (summed * (1.0 / total)).astype(bf16)

    top = score(0)
    for part in range(count):
        after = score(part + 1) if part + 1 < count else None
        finish(part, top)
        top = after

    share = cache_ref.shape[0]
    for k in range(share):
        hit = dest_ref[0] == step * share + k
        decode_ref[k] = jnp.where(hit, arrive_ref[...], cache_ref[k].astype(f32)).astype(bf16)


def attend(length, dest, queries, own, peer, acc, stat, cache, pages, block=1024, sub=256, chunk=256):
    count, width = queries.shape
    latent = 4 * lanes
    keys = 64 * pages
    steps = count // block
    whole = lambda a: pl.BlockSpec(a.shape, lambda i: (0,) * a.ndim)
    strip = lambda w: pl.BlockSpec((block, w), lambda i: (i, 0))
    scalar = pl.BlockSpec(memory_space=pltpu.SMEM)
    share = pl.BlockSpec((cache.shape[0] // steps,) + cache.shape[1:], lambda i: (i, 0, 0))
    return pl.pallas_call(
        functools.partial(attend_kernel, pages, sub, chunk),
        grid=(steps,),
        in_specs=[scalar, scalar, strip(width), whole(own), whole(peer), strip(latent), strip(lanes), share],
        out_specs=[strip(latent), share],
        out_shape=[
            jax.ShapeDtypeStruct((count, latent), bf16),
            jax.ShapeDtypeStruct(cache.shape, bf16),
        ],
        scratch_shapes=[
            pltpu.VMEM((keys, width), bf16),
            pltpu.VMEM((2, sub, keys), f32),
            pltpu.VMEM(cache.shape[1:], f32),
        ],
        compiler_params=pltpu.CompilerParams(vmem_limit_bytes=48 * 1024 * 1024),
        cost_estimate=pl.CostEstimate(
            flops=2 * count * keys * (width + latent), bytes_accessed=20_000_000, transcendentals=count * keys
        ),
    )(length, dest, queries, own, peer, acc, stat, cache)


def body(
    q_latent,
    q_rope,
    new_latent,
    pool_pages,
    page_owner,
    page_slot,
    prefix_len,
    partner,
    dest_slot,
    decode_cache,
):
    stretch, heads, latent = q_latent.shape
    rope = q_rope.shape[1] // heads

    outgoing = spread(partner, pool_pages, new_latent, page_owner, page_slot)
    held = lax.all_to_all(outgoing, "pool", split_axis=0, concat_axis=0, tiled=True)

    token = jnp.arange(stretch, dtype=jnp.int32)
    mark = jnp.broadcast_to(
        (token[:, None] == token[None, :]).astype(bf16)[:, None, :], (stretch, heads, stretch)
    )
    queries = jnp.concatenate([q_latent, q_rope.reshape(stretch, heads, rope), mark], axis=2)
    queries = queries.reshape(stretch * heads, latent + rope + stretch)
    acc, stat = attend_fresh(queries, new_latent)
    held, acc, stat = lax.optimization_barrier((held, acc, stat))

    pages = page_owner.shape[1]
    own = lax.all_to_all(collect(held, pages), "pool", split_axis=0, concat_axis=0, tiled=True)
    peer = lax.ppermute(own, "pd", [(0, 1), (1, 0)])
    context, decode_out = attend(prefix_len, dest_slot, queries, own, peer, acc, stat, decode_cache, pages)
    return (context.reshape(stretch, heads, latent), decode_out)


def solution(mesh):
    placed = (
        P("pool", "pd", None),
        P("pool", "pd"),
        P("pool", None),
        P("pool", None, None),
        P("pool", None),
        P("pool", None),
        P("pool"),
        P("pool"),
        P("pool"),
        P("pool", None, None),
    )
    return jax.shard_map(
        body,
        mesh=mesh,
        in_specs=placed,
        out_specs=(P("pool", "pd", None), P("pool", None, None)),
        check_vma=False,
    )
```

```python
import functools

import jax
import jax.numpy as jnp
from jax import lax
from jax.experimental import pallas as pl
from jax.experimental.pallas import tpu as pltpu
from jax.sharding import PartitionSpec as P

score_scale = 192.0 ** (-0.5)
log2_e = 1.4426950408889634
hidden = -1e30
lanes = 128
f32 = jnp.float32
bf16 = jnp.bfloat16
exchange_rows = 20
reply_rows = 30


def iota(shape, axis):
    return lax.broadcasted_iota(jnp.int32, shape, axis)


def picks(condition):
    return jnp.where(condition, jnp.float32(1.0), jnp.float32(0.0)).astype(bf16)


def mm(a, b):
    return lax.dot_general(a, b, (((1,), (0,)), ((), ())), preferred_element_type=f32)


def mm_first(a, b):
    return lax.dot_general(a, b, (((0,), (0,)), ((), ())), preferred_element_type=f32)


def mm_last(a, b):
    return lax.dot_general(a, b, (((1,), (1,)), ((), ())), preferred_element_type=f32)


def spread_kernel(partner_ref, pages_ref, new_ref, owner_ref, slot_ref, out_ref):
    slots, _, _, rows, width = pages_ref.shape
    core = lax.axis_index("pd")
    held = exchange_rows
    pages = pages_ref[:, core, 0].reshape(slots * rows, width)
    fresh = new_ref[core, 0]
    latent = 4 * lanes
    total = rows * held
    out_row = iota((total, 1), 0)
    out_r = out_row // held
    out_k = out_row % held
    in_row = iota((total, slots * rows), 1)
    in_r = in_row % rows
    in_s = in_row // rows
    same = in_r == out_r
    take_latent = picks(same & (in_s == out_k))
    take_rope = picks(same & (in_s // 8 == out_k - 17))
    new_same = iota((total, rows), 1) == out_r
    take_new = picks(new_same & (out_k == 16))
    take_new_rope = picks(new_same & (out_k == 19))
    src = iota((64, latent), 0)
    dst = iota((64, latent), 1)
    tile = picks((src // 16 == dst // lanes) & (src % 16 == dst % 16))
    group = (iota((slots * rows, latent), 1) % lanes) // 16
    slot = iota((slots * rows, latent), 0) // rows
    rope = mm(pages[:, latent:], tile)
    rope = jnp.where(group == slot % 8, rope, 0.0).astype(bf16)
    first = iota((rows, latent), 1) % lanes < 16
    new_rope = jnp.where(first, mm(fresh[:, latent:], tile), 0.0).astype(bf16)
    result = mm(take_latent, pages[:, :latent]) + mm(take_rope, rope)
    result += mm(take_new, fresh[:, :latent]) + mm(take_new_rope, new_rope)
    asked = owner_ref.shape[1]
    lane = iota((asked, lanes), 1)
    at = iota((asked, lanes), 0)
    meta = mm(owner_ref[...].astype(f32).astype(bf16), picks(lane == at + 32))
    meta += mm(slot_ref[...].astype(f32).astype(bf16), picks(lane == at + 64))
    meta = jnp.where(iota((1, lanes), 1) == 96, partner_ref[0].astype(f32), meta)
    for quarter in range(4):
        part = result[:, quarter * lanes : (quarter + 1) * lanes]
        part = jnp.where(out_k == 19, part + meta, part)
        begin = pl.multiple_of(quarter * 2 * total + pl.program_id(0) * total, total)
        out_ref[pl.ds(begin, total), :] = part.astype(bf16)


def spread(partner, pages, fresh, owner, slot):
    slots, page, width = pages.shape
    rows = page // 4
    whole = lambda a: pl.BlockSpec(a.shape, lambda i: (0,) * a.ndim)
    out = pl.pallas_call(
        spread_kernel,
        grid=(2,),
        in_specs=[
            pl.BlockSpec(memory_space=pltpu.SMEM),
            pl.BlockSpec((slots, 2, 1, rows, width), lambda i: (0, 0, i, 0, 0)),
            pl.BlockSpec((2, 1, rows, width), lambda i: (0, i, 0, 0)),
            whole(owner),
            whole(slot),
        ],
        out_specs=pl.BlockSpec(memory_space=pltpu.VMEM),
        out_shape=jax.ShapeDtypeStruct((8 * rows * exchange_rows, lanes), bf16),
        compiler_params=pltpu.CompilerParams(vmem_limit_bytes=60 * 1024 * 1024),
        cost_estimate=pl.CostEstimate(flops=10**9, bytes_accessed=1_500_000, transcendentals=0),
    )(partner, pages.reshape(slots, 2, 2, rows, width), fresh.reshape(2, 2, rows, width), owner, slot)
    return out.reshape(8 * rows, exchange_rows // 2, 2, lanes)


def collect_kernel(pages, group, all_ref, out_ref, rows_ref, table_ref, stage_ref):
    held = exchange_rows
    owners = all_ref.shape[0] // held
    slots = 16
    size = reply_rows
    rows_ref[...] = all_ref[...].astype(f32)
    src = iota((lanes, lanes), 0)
    dst = iota((lanes, lanes), 1)
    tile = picks(src % 16 == dst % 16)
    lane = iota((owners, lanes), 1)
    for slot in range(slots):
        at = slice(slot * owners, (slot + 1) * owners)
        table_ref[at, :lanes] = rows_ref[pl.ds(slot, owners, stride=held), :].astype(bf16)
        piece = rows_ref[pl.ds(17 + slot // 8, owners, stride=held), :]
        piece = jnp.where(lane // 16 == slot % 8, piece, 0.0).astype(bf16)
        table_ref[at, lanes:] = mm(piece, tile).astype(bf16)
    meta = rows_ref[pl.ds(19, owners, stride=held), :]
    blank = jnp.zeros((owners, lanes), f32)
    ropes = [blank] * (pages // 8)
    for start in range(0, pages, group):
        wanted = []
        for place in range(start, start + group):
            owner = picks(meta[:, 32 + place : 33 + place] == lane.astype(f32))
            slot = jnp.broadcast_to(meta[:, 64 + place : 65 + place], (owners, lanes)).astype(bf16)
            wanted.append(
                jnp.concatenate(
                    [jnp.where(slot == jnp.bfloat16(k), owner, jnp.bfloat16(0)) for k in range(slots)], axis=1
                )
            )
        found = mm(jnp.concatenate(wanted, axis=0), table_ref[...])
        for k in range(group):
            place = start + k
            got = found[k * owners : (k + 1) * owners]
            stage_ref[pl.ds(place, owners, stride=size), :] = got[:, :lanes]
            ropes[place // 8] += jnp.where(lane // 16 == place % 8, got[:, lanes:], 0.0)
    comes = picks(meta[:, 96:97].astype(jnp.int32) == lane)
    arriving = mm_first(comes, rows_ref[pl.ds(16, owners, stride=held), :].astype(bf16))
    arriving_rope = mm_first(comes, jnp.where(lane < 16, meta, 0.0).astype(bf16))
    tail = [arriving] + ropes + [arriving_rope]
    tail += [blank] * (size - pages - len(tail))
    for k, piece in enumerate(tail):
        stage_ref[pl.ds(pages + k, owners, stride=size), :] = piece
    out_ref[...] = stage_ref[...].astype(bf16)


def collect(held, pages):
    owners = held.shape[0]
    held = held.reshape(owners * exchange_rows, lanes)
    out = pl.pallas_call(
        functools.partial(collect_kernel, pages, 4),
        in_specs=[pl.BlockSpec(memory_space=pltpu.VMEM)],
        out_specs=pl.BlockSpec(memory_space=pltpu.VMEM),
        out_shape=jax.ShapeDtypeStruct((owners * reply_rows, lanes), bf16),
        scratch_shapes=[
            pltpu.VMEM(held.shape, f32),
            pltpu.VMEM((owners * 16, 2 * lanes), bf16),
            pltpu.VMEM((owners * reply_rows, lanes), f32),
        ],
        compiler_params=pltpu.CompilerParams(vmem_limit_bytes=40 * 1024 * 1024),
        cost_estimate=pl.CostEstimate(flops=4 * 10**9, bytes_accessed=1_500_000, transcendentals=0),
    )(held)
    return out.reshape(owners, reply_rows // 2, 2, lanes)


factor = score_scale * log2_e


def fresh_kernel(sub, q_ref, new_ref, acc_ref, stat_ref, value_ref, key_ref):
    latent = 4 * lanes

    @pl.when(pl.program_id(0) == 0)
    def build():
        fresh = new_ref[...].astype(f32)
        part = jnp.concatenate([fresh[:, :latent], jnp.zeros((64, latent), f32)], axis=0)
        value_ref[...] = part.astype(bf16)
        key_ref[:latent, :] = part.T.astype(bf16)
        rope = jnp.concatenate([fresh[:, latent:], jnp.zeros((64, 64), f32)], axis=0)
        key_ref[latent : latent + 64, :] = rope.T.astype(bf16)
        token = iota((64, lanes), 0)
        late = iota((64, lanes), 1)
        key_ref[latent + 64 :, :] = jnp.where(late <= token, 0.0, hidden).astype(bf16)

    for part in range(q_ref.shape[0] // sub):
        at = slice(part * sub, (part + 1) * sub)
        scores = mm(q_ref[at, :], key_ref[...])
        top = jnp.max(scores, axis=1, keepdims=True)
        weight = jnp.exp2((scores - top) * jnp.float32(factor))
        total = jnp.sum(weight, axis=1, keepdims=True)
        acc_ref[at, :] = mm(weight.astype(bf16), value_ref[...])
        stat_ref[at, :] = jnp.where(iota((sub, lanes), 1) < 64, top, total)


def attend_fresh(queries, fresh, block=512, sub=256):
    count, width = queries.shape
    latent = 4 * lanes
    return pl.pallas_call(
        functools.partial(fresh_kernel, sub),
        grid=(count // block,),
        in_specs=[
            pl.BlockSpec((block, width), lambda i: (i, 0)),
            pl.BlockSpec(fresh.shape, lambda i: (0, 0)),
        ],
        out_specs=[
            pl.BlockSpec((block, latent), lambda i: (i, 0)),
            pl.BlockSpec((block, lanes), lambda i: (i, 0)),
        ],
        out_shape=[
            jax.ShapeDtypeStruct((count, latent), f32),
            jax.ShapeDtypeStruct((count, lanes), f32),
        ],
        scratch_shapes=[pltpu.VMEM((lanes, latent), bf16), pltpu.VMEM((width, lanes), bf16)],
        compiler_params=pltpu.CompilerParams(vmem_limit_bytes=40 * 1024 * 1024),
        cost_estimate=pl.CostEstimate(flops=5 * 10**9, bytes_accessed=16_000_000, transcendentals=count * lanes),
    )(queries, fresh)


def attend_kernel(
    pages,
    sub,
    chunk,
    length_ref,
    dest_ref,
    q_ref,
    own_ref,
    peer_ref,
    acc_ref,
    stat_ref,
    cache_ref,
    out_ref,
    decode_ref,
    key_ref,
    score_ref,
    arrive_ref,
    rows_ref,
):
    latent = 4 * lanes
    size = reply_rows
    rows = own_ref.shape[0] // (4 * size)
    half = rows * pages
    keys = 2 * half
    step = pl.program_id(0)

    @pl.when(step == 0)
    def build():
        core = lax.axis_index("pd")
        src = iota((lanes, lanes), 0)
        dst = iota((lanes, lanes), 1)
        lane = iota((rows, lanes), 1)
        key = iota((half, 1), 0)
        place = (key // rows) * 64 + key % rows
        for side, ref in enumerate((own_ref, peer_ref)):
            at = slice(side * half, (side + 1) * half)
            spot = pl.multiple_of((core if side == 0 else 1 - core) * rows, rows)
            rope_keys = jnp.zeros((half, lanes), f32)
            arrived_rope = jnp.zeros((rows, lanes), f32)
            rows_ref[...] = ref[...].astype(f32)
            for quarter in range(4):
                cols = slice(quarter * lanes, (quarter + 1) * lanes)
                take = lambda k: rows_ref[pl.ds(quarter * rows * size + k, rows, stride=size), :]
                for k in range(pages):
                    begin = side * half + k * rows
                    key_ref[begin : begin + rows, cols] = take(k).astype(bf16)
                ropes = [take(pages + 1 + k) for k in range(pages // 8)]
                pieces = [jnp.where(lane // 16 == k % 8, ropes[k // 8], 0.0) for k in range(pages)]
                rope = jnp.concatenate(pieces, axis=0).astype(bf16)
                put = picks((dst // 16 == quarter) & (dst % 16 == src % 16))
                rope_keys += mm(rope, put)
                arrive_ref[pl.ds(spot, rows), cols] = take(pages)
                last = jnp.where(lane < 16, take(pages + 1 + pages // 8), 0.0)
                arrived_rope += mm(last.astype(bf16), put)
            arrive_ref[pl.ds(spot, rows), latent:] = arrived_rope[:, :64]
            bias = jnp.where(place + spot < length_ref[0], 0.0, hidden)
            joined = jnp.where(iota((half, lanes), 1) < 64, rope_keys, bias)
            key_ref[at, latent:] = joined.astype(bf16)

    count = q_ref.shape[0] // sub
    scale = jnp.float32(factor)

    def score(part):
        at = slice(part * sub, (part + 1) * sub)
        top = None
        for begin in range(0, keys, chunk):
            found = mm_last(q_ref[at, :], key_ref[begin : begin + chunk, :])
            score_ref[part % 2, :, begin : begin + chunk] = found
            for k in range(0, chunk, lanes):
                piece = found[:, k : k + lanes]
                top = piece if top is None else jnp.maximum(top, piece)
        return jnp.maximum(jnp.max(top, axis=1, keepdims=True), stat_ref[at, :1])

    def finish(part, top):
        at = slice(part * sub, (part + 1) * sub)
        summed = None
        total = None
        for begin in range(0, keys, chunk):
            weight = jnp.exp2((score_ref[part % 2, :, begin : begin + chunk] - top) * scale)
            for k in range(0, chunk, lanes):
                piece = weight[:, k : k + lanes]
                total = piece if total is None else total + piece
            product = mm(weight.astype(bf16), key_ref[begin : begin + chunk, :latent])
            summed = product if summed is None else summed + product
        shrink = jnp.exp2((stat_ref[at, :1] - top) * scale)
        total = jnp.sum(total, axis=1, keepdims=True) + shrink * stat_ref[at, 64:65]
        summed = summed + shrink * acc_ref[at, :]
        out_ref[at, :] = (summed * (1.0 / total)).astype(bf16)

    top = score(0)
    for part in range(count):
        after = score(part + 1) if part + 1 < count else None
        finish(part, top)
        top = after

    share = cache_ref.shape[0]
    for k in range(share):
        hit = dest_ref[0] == step * share + k
        decode_ref[k] = jnp.where(hit, arrive_ref[...], cache_ref[k].astype(f32)).astype(bf16)


def attend(length, dest, queries, own, peer, acc, stat, cache, pages, block=1024, sub=256, chunk=256):
    count, width = queries.shape
    latent = 4 * lanes
    keys = 64 * pages
    steps = count // block
    whole = lambda a: pl.BlockSpec(a.shape, lambda i: (0,) * a.ndim)
    strip = lambda w: pl.BlockSpec((block, w), lambda i: (i, 0))
    scalar = pl.BlockSpec(memory_space=pltpu.SMEM)
    share = pl.BlockSpec((cache.shape[0] // steps,) + cache.shape[1:], lambda i: (i, 0, 0))
    return pl.pallas_call(
        functools.partial(attend_kernel, pages, sub, chunk),
        grid=(steps,),
        in_specs=[scalar, scalar, strip(width), whole(own), whole(peer), strip(latent), strip(lanes), share],
        out_specs=[strip(latent), share],
        out_shape=[
            jax.ShapeDtypeStruct((count, latent), bf16),
            jax.ShapeDtypeStruct(cache.shape, bf16),
        ],
        scratch_shapes=[
            pltpu.VMEM((keys, width), bf16),
            pltpu.VMEM((2, sub, keys), f32),
            pltpu.VMEM(cache.shape[1:], f32),
            pltpu.VMEM(own.shape, f32),
        ],
        compiler_params=pltpu.CompilerParams(vmem_limit_bytes=48 * 1024 * 1024),
        cost_estimate=pl.CostEstimate(
            flops=2 * count * keys * (width + latent), bytes_accessed=20_000_000, transcendentals=count * keys
        ),
    )(length, dest, queries, own, peer, acc, stat, cache)


def body(
    q_latent,
    q_rope,
    new_latent,
    pool_pages,
    page_owner,
    page_slot,
    prefix_len,
    partner,
    dest_slot,
    decode_cache,
):
    stretch, heads, latent = q_latent.shape
    rope = q_rope.shape[1] // heads

    outgoing = spread(partner, pool_pages, new_latent, page_owner, page_slot)
    held = lax.all_to_all(outgoing, "pool", split_axis=0, concat_axis=0, tiled=True)

    token = jnp.arange(stretch, dtype=jnp.int32)
    mark = jnp.broadcast_to(
        (token[:, None] == token[None, :]).astype(bf16)[:, None, :], (stretch, heads, stretch)
    )
    queries = jnp.concatenate([q_latent, q_rope.reshape(stretch, heads, rope), mark], axis=2)
    queries = queries.reshape(stretch * heads, latent + rope + stretch)
    acc, stat = attend_fresh(queries, new_latent)
    held, acc, stat = lax.optimization_barrier((held, acc, stat))

    pages = page_owner.shape[1]
    own = lax.all_to_all(collect(held, pages), "pool", split_axis=0, concat_axis=0, tiled=True)
    own = own.reshape(-1, lanes)
    peer = lax.ppermute(own, "pd", [(0, 1), (1, 0)])
    context, decode_out = attend(prefix_len, dest_slot, queries, own, peer, acc, stat, decode_cache, pages)
    return (context.reshape(stretch, heads, latent), decode_out)


def solution(mesh):
    placed = (
        P("pool", "pd", None),
        P("pool", "pd"),
        P("pool", None),
        P("pool", None, None),
        P("pool", None),
        P("pool", None),
        P("pool"),
        P("pool"),
        P("pool"),
        P("pool", None, None),
    )
    return jax.shard_map(
        body,
        mesh=mesh,
        in_specs=placed,
        out_specs=(P("pool", "pd", None), P("pool", None, None)),
        check_vma=False,
    )
```

```python
import functools

import jax
import jax.numpy as jnp
from jax import lax
from jax.experimental import pallas as pl
from jax.experimental.pallas import tpu as pltpu
from jax.sharding import PartitionSpec as P

score_scale = 192.0 ** (-0.5)
log2_e = 1.4426950408889634
hidden = -1e30
lanes = 128
f32 = jnp.float32
bf16 = jnp.bfloat16
exchange_rows = 20
reply_rows = 30


def iota(shape, axis):
    return lax.broadcasted_iota(jnp.int32, shape, axis)


def picks(condition):
    return jnp.where(condition, jnp.float32(1.0), jnp.float32(0.0)).astype(bf16)


def mm(a, b):
    return lax.dot_general(a, b, (((1,), (0,)), ((), ())), preferred_element_type=f32)


def mm_first(a, b):
    return lax.dot_general(a, b, (((0,), (0,)), ((), ())), preferred_element_type=f32)


def mm_last(a, b):
    return lax.dot_general(a, b, (((1,), (1,)), ((), ())), preferred_element_type=f32)


def spread_kernel(partner_ref, pages_ref, new_ref, owner_ref, slot_ref, out_ref):
    slots, _, _, rows, width = pages_ref.shape
    core = lax.axis_index("pd")
    held = exchange_rows
    pages = pages_ref[:, core, 0].reshape(slots * rows, width)
    fresh = new_ref[core, 0]
    latent = 4 * lanes
    total = rows * held
    out_row = iota((total, 1), 0)
    out_r = (out_row * 3277) >> 16
    out_k = out_row - out_r * held
    in_row = iota((total, slots * rows), 1)
    shift = rows.bit_length() - 1
    in_r = in_row & (rows - 1)
    in_s = in_row >> shift
    same = in_r == out_r
    take_latent = picks(same & (in_s == out_k))
    take_rope = picks(same & ((in_s >> 3) == out_k - 17))
    new_same = iota((total, rows), 1) == out_r
    take_new = picks(new_same & (out_k == 16))
    take_new_rope = picks(new_same & (out_k == 19))
    src = iota((64, latent), 0)
    dst = iota((64, latent), 1)
    tile = picks(((src >> 4) == (dst >> 7)) & ((src & 15) == (dst & 15)))
    group = (iota((slots * rows, latent), 1) >> 4) & 7
    slot = iota((slots * rows, latent), 0) >> shift
    rope = mm(pages[:, latent:], tile)
    rope = jnp.where(group == (slot & 7), rope, 0.0).astype(bf16)
    first = (iota((rows, latent), 1) & (lanes - 1)) < 16
    new_rope = jnp.where(first, mm(fresh[:, latent:], tile), 0.0).astype(bf16)
    result = mm(take_latent, pages[:, :latent]) + mm(take_rope, rope)
    result += mm(take_new, fresh[:, :latent]) + mm(take_new_rope, new_rope)
    asked = owner_ref.shape[1]
    lane = iota((asked, lanes), 1)
    at = iota((asked, lanes), 0)
    meta = mm(owner_ref[...].astype(f32).astype(bf16), picks(lane == at + 32))
    meta += mm(slot_ref[...].astype(f32).astype(bf16), picks(lane == at + 64))
    meta = jnp.where(iota((1, lanes), 1) == 96, partner_ref[0].astype(f32), meta)
    for quarter in range(4):
        part = result[:, quarter * lanes : (quarter + 1) * lanes]
        part = jnp.where(out_k == 19, part + meta, part)
        begin = pl.multiple_of(quarter * 2 * total + pl.program_id(0) * total, total)
        out_ref[pl.ds(begin, total), :] = part.astype(bf16)


def spread(partner, pages, fresh, owner, slot):
    slots, page, width = pages.shape
    rows = page // 4
    whole = lambda a: pl.BlockSpec(a.shape, lambda i: (0,) * a.ndim)
    out = pl.pallas_call(
        spread_kernel,
        grid=(2,),
        in_specs=[
            pl.BlockSpec(memory_space=pltpu.SMEM),
            pl.BlockSpec((slots, 2, 1, rows, width), lambda i: (0, 0, i, 0, 0)),
            pl.BlockSpec((2, 1, rows, width), lambda i: (0, i, 0, 0)),
            whole(owner),
            whole(slot),
        ],
        out_specs=pl.BlockSpec(memory_space=pltpu.VMEM),
        out_shape=jax.ShapeDtypeStruct((8 * rows * exchange_rows, lanes), bf16),
        compiler_params=pltpu.CompilerParams(vmem_limit_bytes=60 * 1024 * 1024),
        cost_estimate=pl.CostEstimate(flops=10**9, bytes_accessed=1_500_000, transcendentals=0),
    )(partner, pages.reshape(slots, 2, 2, rows, width), fresh.reshape(2, 2, rows, width), owner, slot)
    return out.reshape(8 * rows, exchange_rows // 2, 2, lanes)


def collect_kernel(pages, group, all_ref, out_ref, rows_ref, table_ref, stage_ref):
    held = exchange_rows
    owners = all_ref.shape[0] // held
    slots = 16
    size = reply_rows
    rows_ref[...] = all_ref[...].astype(f32)
    src = iota((lanes, lanes), 0)
    dst = iota((lanes, lanes), 1)
    tile = picks((src & 15) == (dst & 15))
    lane = iota((owners, lanes), 1)
    for slot in range(slots):
        at = slice(slot * owners, (slot + 1) * owners)
        table_ref[at, :lanes] = rows_ref[pl.ds(slot, owners, stride=held), :].astype(bf16)
        piece = rows_ref[pl.ds(17 + slot // 8, owners, stride=held), :]
        piece = jnp.where((lane >> 4) == slot % 8, piece, 0.0).astype(bf16)
        table_ref[at, lanes:] = mm(piece, tile).astype(bf16)
    meta = rows_ref[pl.ds(19, owners, stride=held), :]
    blank = jnp.zeros((owners, lanes), f32)
    ropes = [blank] * (pages // 8)
    for start in range(0, pages, group):
        wanted = []
        for place in range(start, start + group):
            owner = picks(meta[:, 32 + place : 33 + place] == lane.astype(f32))
            slot = jnp.broadcast_to(meta[:, 64 + place : 65 + place], (owners, lanes)).astype(bf16)
            wanted.append(
                jnp.concatenate(
                    [jnp.where(slot == jnp.bfloat16(k), owner, jnp.bfloat16(0)) for k in range(slots)], axis=1
                )
            )
        found = mm(jnp.concatenate(wanted, axis=0), table_ref[...])
        for k in range(group):
            place = start + k
            got = found[k * owners : (k + 1) * owners]
            stage_ref[pl.ds(place, owners, stride=size), :] = got[:, :lanes]
            ropes[place // 8] += jnp.where((lane >> 4) == place % 8, got[:, lanes:], 0.0)
    comes = picks(meta[:, 96:97].astype(jnp.int32) == lane)
    arriving = mm_first(comes, rows_ref[pl.ds(16, owners, stride=held), :].astype(bf16))
    arriving_rope = mm_first(comes, jnp.where(lane < 16, meta, 0.0).astype(bf16))
    tail = [arriving] + ropes + [arriving_rope]
    tail += [blank] * (size - pages - len(tail))
    for k, piece in enumerate(tail):
        stage_ref[pl.ds(pages + k, owners, stride=size), :] = piece
    out_ref[...] = stage_ref[...].astype(bf16)


def collect(held, pages):
    owners = held.shape[0]
    held = held.reshape(owners * exchange_rows, lanes)
    out = pl.pallas_call(
        functools.partial(collect_kernel, pages, 4),
        in_specs=[pl.BlockSpec(memory_space=pltpu.VMEM)],
        out_specs=pl.BlockSpec(memory_space=pltpu.VMEM),
        out_shape=jax.ShapeDtypeStruct((owners * reply_rows, lanes), bf16),
        scratch_shapes=[
            pltpu.VMEM(held.shape, f32),
            pltpu.VMEM((owners * 16, 2 * lanes), bf16),
            pltpu.VMEM((owners * reply_rows, lanes), f32),
        ],
        compiler_params=pltpu.CompilerParams(vmem_limit_bytes=40 * 1024 * 1024),
        cost_estimate=pl.CostEstimate(flops=4 * 10**9, bytes_accessed=1_500_000, transcendentals=0),
    )(held)
    return out.reshape(owners, reply_rows // 2, 2, lanes)


factor = score_scale * log2_e


def joined(latent_ref, rope_ref, at):
    return jnp.concatenate([latent_ref[at, :], rope_ref[at, :]], axis=1)


def fresh_kernel(sub, q_ref, rope_ref, new_ref, acc_ref, stat_ref, value_ref, key_ref):
    latent = 4 * lanes

    @pl.when(pl.program_id(0) == 0)
    def build():
        fresh = new_ref[...].astype(f32)
        part = jnp.concatenate([fresh[:, :latent], jnp.zeros((64, latent), f32)], axis=0)
        value_ref[...] = part.astype(bf16)
        key_ref[:latent, :] = part.T.astype(bf16)
        rope = jnp.concatenate([fresh[:, latent:], jnp.zeros((64, 64), f32)], axis=0)
        key_ref[latent : latent + 64, :] = rope.T.astype(bf16)
        token = iota((64, lanes), 0)
        late = iota((64, lanes), 1)
        key_ref[latent + 64 :, :] = jnp.where(late <= token, 0.0, hidden).astype(bf16)

    for part in range(q_ref.shape[0] // sub):
        at = slice(part * sub, (part + 1) * sub)
        scores = mm(joined(q_ref, rope_ref, at), key_ref[...])
        top = jnp.max(scores, axis=1, keepdims=True)
        weight = jnp.exp2((scores - top) * jnp.float32(factor))
        total = jnp.sum(weight, axis=1, keepdims=True)
        acc_ref[at, :] = mm(weight.astype(bf16), value_ref[...])
        stat_ref[at, :] = jnp.where(iota((sub, lanes), 1) < 64, top, total)


def attend_fresh(queries, ropes, fresh, block=1024, sub=256):
    count, latent = queries.shape
    width = latent + lanes
    return pl.pallas_call(
        functools.partial(fresh_kernel, sub),
        grid=(count // block,),
        in_specs=[
            pl.BlockSpec((block, latent), lambda i: (i, 0)),
            pl.BlockSpec((block, lanes), lambda i: (i, 0)),
            pl.BlockSpec(fresh.shape, lambda i: (0, 0)),
        ],
        out_specs=[
            pl.BlockSpec((block, latent), lambda i: (i, 0)),
            pl.BlockSpec((block, lanes), lambda i: (i, 0)),
        ],
        out_shape=[
            jax.ShapeDtypeStruct((count, latent), f32),
            jax.ShapeDtypeStruct((count, lanes), f32),
        ],
        scratch_shapes=[pltpu.VMEM((lanes, latent), bf16), pltpu.VMEM((width, lanes), bf16)],
        compiler_params=pltpu.CompilerParams(vmem_limit_bytes=40 * 1024 * 1024),
        cost_estimate=pl.CostEstimate(flops=5 * 10**9, bytes_accessed=16_000_000, transcendentals=count * lanes),
    )(queries, ropes, fresh)


def unpack(pages, spot, length, ref, rows_ref, key_ref, arrive_ref):
    latent = 4 * lanes
    size = reply_rows
    rows = ref.shape[0] // (4 * size)
    half = rows * pages
    shift = rows.bit_length() - 1
    src = iota((lanes, lanes), 0)
    dst = iota((lanes, lanes), 1)
    lane = iota((rows, lanes), 1)
    rope_keys = jnp.zeros((half, lanes), f32)
    arrived_rope = jnp.zeros((rows, lanes), f32)
    rows_ref[...] = ref[...].astype(f32)
    for quarter in range(4):
        cols = slice(quarter * lanes, (quarter + 1) * lanes)
        take = lambda k: rows_ref[pl.ds(quarter * rows * size + k, rows, stride=size), :]
        for k in range(pages):
            key_ref[k * rows : (k + 1) * rows, cols] = take(k).astype(bf16)
        ropes = [take(pages + 1 + k) for k in range(pages // 8)]
        pieces = [jnp.where((lane >> 4) == k % 8, ropes[k // 8], 0.0) for k in range(pages)]
        rope = jnp.concatenate(pieces, axis=0).astype(bf16)
        put = picks(((dst >> 4) == quarter) & ((dst & 15) == (src & 15)))
        rope_keys += mm(rope, put)
        arrive_ref[:, cols] = take(pages)
        last = jnp.where(lane < 16, take(pages + 1 + pages // 8), 0.0)
        arrived_rope += mm(last.astype(bf16), put)
    arrive_ref[:, latent:] = arrived_rope[:, :64]
    key = iota((half, lanes), 0)
    place = (key >> shift) * 64 + (key & (rows - 1)) + spot
    bias = jnp.where(place < length, 0.0, hidden)
    extra = jnp.where(iota((half, lanes), 1) < 64, rope_keys, bias)
    key_ref[:, latent:] = extra.astype(bf16)


def unpack_kernel(pages, length_ref, own_ref, key_ref, arrive_ref, rows_ref):
    spot = lax.axis_index("pd") * (own_ref.shape[0] // (4 * reply_rows))
    unpack(pages, spot, length_ref[0], own_ref, rows_ref, key_ref, arrive_ref)


def unpack_own(length, own, pages, width):
    rows = own.shape[0] // (4 * reply_rows)
    inside = pl.BlockSpec(memory_space=pltpu.VMEM)
    return pl.pallas_call(
        functools.partial(unpack_kernel, pages),
        in_specs=[pl.BlockSpec(memory_space=pltpu.SMEM), inside],
        out_specs=[inside, inside],
        out_shape=[
            jax.ShapeDtypeStruct((rows * pages, 5 * lanes), bf16),
            jax.ShapeDtypeStruct((rows, width), f32),
        ],
        scratch_shapes=[pltpu.VMEM(own.shape, f32)],
        compiler_params=pltpu.CompilerParams(vmem_limit_bytes=40 * 1024 * 1024),
        cost_estimate=pl.CostEstimate(flops=10**9, bytes_accessed=2_000_000, transcendentals=0),
    )(length, own)


def attend_kernel(
    pages,
    sub,
    chunk,
    length_ref,
    dest_ref,
    q_ref,
    rope_ref,
    own_ref,
    mine_ref,
    peer_ref,
    acc_ref,
    stat_ref,
    cache_ref,
    out_ref,
    decode_ref,
    key_ref,
    score_ref,
    arrive_ref,
    rows_ref,
):
    latent = 4 * lanes
    rows = mine_ref.shape[0]
    half = rows * pages
    keys = 2 * half
    step = pl.program_id(0)

    def key_block(begin, cols):
        ref, at = (own_ref, begin) if begin < half else (key_ref, begin - half)
        return ref[at : at + chunk, cols]

    @pl.when(step == 0)
    def build():
        core = lax.axis_index("pd")
        spot = pl.multiple_of(core * rows, rows)
        other = pl.multiple_of((1 - core) * rows, rows)
        arrive_ref[pl.ds(spot, rows), :] = mine_ref[...]
        unpack(pages, other, length_ref[0], peer_ref, rows_ref, key_ref, arrive_ref.at[pl.ds(other, rows), :])

    count = q_ref.shape[0] // sub
    scale = jnp.float32(factor)

    def score(part):
        at = slice(part * sub, (part + 1) * sub)
        query = joined(q_ref, rope_ref, at)
        top = None
        for begin in range(0, keys, chunk):
            found = mm_last(query, key_block(begin, slice(None)))
            score_ref[part % 2, :, begin : begin + chunk] = found
            for k in range(0, chunk, lanes):
                piece = found[:, k : k + lanes]
                top = piece if top is None else jnp.maximum(top, piece)
        return jnp.maximum(jnp.max(top, axis=1, keepdims=True), stat_ref[at, :1])

    def finish(part, top):
        at = slice(part * sub, (part + 1) * sub)
        summed = None
        total = None
        for begin in range(0, keys, chunk):
            weight = jnp.exp2((score_ref[part % 2, :, begin : begin + chunk] - top) * scale)
            for k in range(0, chunk, lanes):
                piece = weight[:, k : k + lanes]
                total = piece if total is None else total + piece
            product = mm(weight.astype(bf16), key_block(begin, slice(0, latent)))
            summed = product if summed is None else summed + product
        shrink = jnp.exp2((stat_ref[at, :1] - top) * scale)
        total = jnp.sum(total, axis=1, keepdims=True) + shrink * stat_ref[at, 64:65]
        summed = summed + shrink * acc_ref[at, :]
        out_ref[at, :] = (summed * (1.0 / total)).astype(bf16)

    top = score(0)
    for part in range(count):
        after = score(part + 1) if part + 1 < count else None
        finish(part, top)
        top = after

    share = cache_ref.shape[0]
    for k in range(share):
        hit = dest_ref[0] == step * share + k
        decode_ref[k] = jnp.where(hit, arrive_ref[...], cache_ref[k].astype(f32)).astype(bf16)


def attend(length, dest, queries, ropes, own, mine, peer, acc, stat, cache, pages, block=1024, sub=256, chunk=256):
    count, latent = queries.shape
    width = latent + lanes
    keys = 64 * pages
    steps = count // block
    whole = lambda a: pl.BlockSpec(a.shape, lambda i: (0,) * a.ndim)
    strip = lambda w: pl.BlockSpec((block, w), lambda i: (i, 0))
    scalar = pl.BlockSpec(memory_space=pltpu.SMEM)
    share = pl.BlockSpec((cache.shape[0] // steps,) + cache.shape[1:], lambda i: (i, 0, 0))
    return pl.pallas_call(
        functools.partial(attend_kernel, pages, sub, chunk),
        grid=(steps,),
        in_specs=[scalar, scalar, strip(latent), strip(lanes), whole(own), whole(mine), whole(peer), strip(latent), strip(lanes), share],
        out_specs=[strip(latent), share],
        out_shape=[
            jax.ShapeDtypeStruct((count, latent), bf16),
            jax.ShapeDtypeStruct(cache.shape, bf16),
        ],
        scratch_shapes=[
            pltpu.VMEM((keys // 2, width), bf16),
            pltpu.VMEM((2, sub, keys), f32),
            pltpu.VMEM(cache.shape[1:], f32),
            pltpu.VMEM(peer.shape, f32),
        ],
        compiler_params=pltpu.CompilerParams(vmem_limit_bytes=48 * 1024 * 1024),
        cost_estimate=pl.CostEstimate(
            flops=2 * count * keys * (width + latent), bytes_accessed=20_000_000, transcendentals=count * keys
        ),
    )(length, dest, queries, ropes, own, mine, peer, acc, stat, cache)


def body(
    q_latent,
    q_rope,
    new_latent,
    pool_pages,
    page_owner,
    page_slot,
    prefix_len,
    partner,
    dest_slot,
    decode_cache,
):
    stretch, heads, latent = q_latent.shape
    rope = q_rope.shape[1] // heads

    outgoing = spread(partner, pool_pages, new_latent, page_owner, page_slot)
    held = lax.all_to_all(outgoing, "pool", split_axis=0, concat_axis=0, tiled=True)

    token = jnp.arange(stretch, dtype=jnp.int32)
    mark = jnp.broadcast_to(
        (token[:, None] == token[None, :]).astype(bf16)[:, None, :], (stretch, heads, stretch)
    )
    ropes = jnp.concatenate([q_rope.reshape(stretch, heads, rope), mark], axis=2)
    ropes = ropes.reshape(stretch * heads, lanes)
    queries = q_latent.reshape(stretch * heads, latent)
    acc, stat = attend_fresh(queries, ropes, new_latent)
    held, acc, stat = lax.optimization_barrier((held, acc, stat))

    pages = page_owner.shape[1]
    own = lax.all_to_all(collect(held, pages), "pool", split_axis=0, concat_axis=0, tiled=True)
    own = own.reshape(-1, lanes)
    peer = lax.ppermute(own, "pd", [(0, 1), (1, 0)])
    own, mine = unpack_own(prefix_len, own, pages, new_latent.shape[1])
    context, decode_out = attend(prefix_len, dest_slot, queries, ropes, own, mine, peer, acc, stat, decode_cache, pages)
    return (context.reshape(stretch, heads, latent), decode_out)


def solution(mesh):
    placed = (
        P("pool", "pd", None),
        P("pool", "pd"),
        P("pool", None),
        P("pool", None, None),
        P("pool", None),
        P("pool", None),
        P("pool"),
        P("pool"),
        P("pool"),
        P("pool", None, None),
    )
    return jax.shard_map(
        body,
        mesh=mesh,
        in_specs=placed,
        out_specs=(P("pool", "pd", None), P("pool", None, None)),
        check_vma=False,
    )
```

```python
import functools

import jax
import jax.numpy as jnp
from jax import lax
from jax.experimental import pallas as pl
from jax.experimental.pallas import tpu as pltpu
from jax.sharding import PartitionSpec as P

score_scale = 192.0 ** (-0.5)
log2_e = 1.4426950408889634
hidden = -1e30
lanes = 128
f32 = jnp.float32
bf16 = jnp.bfloat16
exchange_rows = 20
reply_rows = 30


def iota(shape, axis):
    return lax.broadcasted_iota(jnp.int32, shape, axis)


def picks(condition):
    return jnp.where(condition, jnp.float32(1.0), jnp.float32(0.0)).astype(bf16)


def mm(a, b):
    return lax.dot_general(a, b, (((1,), (0,)), ((), ())), preferred_element_type=f32)


def mm_first(a, b):
    return lax.dot_general(a, b, (((0,), (0,)), ((), ())), preferred_element_type=f32)


def mm_last(a, b):
    return lax.dot_general(a, b, (((1,), (1,)), ((), ())), preferred_element_type=f32)


def spread_kernel(partner_ref, pages_ref, new_ref, owner_ref, slot_ref, out_ref):
    slots, _, _, rows, width = pages_ref.shape
    core = lax.axis_index("pd")
    held = exchange_rows
    pages = pages_ref[:, core, 0].reshape(slots * rows, width)
    fresh = new_ref[core, 0]
    latent = 4 * lanes
    total = rows * held
    out_row = iota((total, 1), 0)
    out_r = (out_row * 3277) >> 16
    out_k = out_row - out_r * held
    in_row = iota((total, slots * rows), 1)
    shift = rows.bit_length() - 1
    in_r = in_row & (rows - 1)
    in_s = in_row >> shift
    same = in_r == out_r
    take_latent = picks(same & (in_s == out_k))
    take_rope = picks(same & ((in_s >> 3) == out_k - 17))
    new_same = iota((total, rows), 1) == out_r
    take_new = picks(new_same & (out_k == 16))
    take_new_rope = picks(new_same & (out_k == 19))
    src = iota((64, latent), 0)
    dst = iota((64, latent), 1)
    tile = picks(((src >> 4) == (dst >> 7)) & ((src & 15) == (dst & 15)))
    group = (iota((slots * rows, latent), 1) >> 4) & 7
    slot = iota((slots * rows, latent), 0) >> shift
    rope = mm(pages[:, latent:], tile)
    rope = jnp.where(group == (slot & 7), rope, 0.0).astype(bf16)
    first = (iota((rows, latent), 1) & (lanes - 1)) < 16
    new_rope = jnp.where(first, mm(fresh[:, latent:], tile), 0.0).astype(bf16)
    result = mm(take_latent, pages[:, :latent]) + mm(take_rope, rope)
    result += mm(take_new, fresh[:, :latent]) + mm(take_new_rope, new_rope)
    asked = owner_ref.shape[1]
    lane = iota((asked, lanes), 1)
    at = iota((asked, lanes), 0)
    meta = mm(owner_ref[...].astype(f32).astype(bf16), picks(lane == at + 32))
    meta += mm(slot_ref[...].astype(f32).astype(bf16), picks(lane == at + 64))
    meta = jnp.where(iota((1, lanes), 1) == 96, partner_ref[0].astype(f32), meta)
    for quarter in range(4):
        part = result[:, quarter * lanes : (quarter + 1) * lanes]
        part = jnp.where(out_k == 19, part + meta, part)
        begin = pl.multiple_of(quarter * 2 * total + pl.program_id(0) * total, total)
        out_ref[pl.ds(begin, total), :] = part.astype(bf16)


def spread(partner, pages, fresh, owner, slot):
    slots, page, width = pages.shape
    rows = page // 4
    whole = lambda a: pl.BlockSpec(a.shape, lambda i: (0,) * a.ndim)
    out = pl.pallas_call(
        spread_kernel,
        grid=(2,),
        in_specs=[
            pl.BlockSpec(memory_space=pltpu.SMEM),
            pl.BlockSpec((slots, 2, 1, rows, width), lambda i: (0, 0, i, 0, 0)),
            pl.BlockSpec((2, 1, rows, width), lambda i: (0, i, 0, 0)),
            whole(owner),
            whole(slot),
        ],
        out_specs=pl.BlockSpec(memory_space=pltpu.VMEM),
        out_shape=jax.ShapeDtypeStruct((8 * rows * exchange_rows, lanes), bf16),
        compiler_params=pltpu.CompilerParams(vmem_limit_bytes=60 * 1024 * 1024),
        cost_estimate=pl.CostEstimate(flops=10**9, bytes_accessed=1_500_000, transcendentals=0),
    )(partner, pages.reshape(slots, 2, 2, rows, width), fresh.reshape(2, 2, rows, width), owner, slot)
    return out.reshape(8 * rows, exchange_rows // 2, 2, lanes)


def collect_kernel(pages, group, all_ref, out_ref, rows_ref, table_ref, stage_ref):
    held = exchange_rows
    owners = all_ref.shape[0] // held
    slots = 16
    size = reply_rows
    rows_ref[...] = all_ref[...].astype(f32)
    src = iota((lanes, lanes), 0)
    dst = iota((lanes, lanes), 1)
    tile = picks((src & 15) == (dst & 15))
    lane = iota((owners, lanes), 1)
    for slot in range(slots):
        at = slice(slot * owners, (slot + 1) * owners)
        table_ref[at, :lanes] = rows_ref[pl.ds(slot, owners, stride=held), :].astype(bf16)
        piece = rows_ref[pl.ds(17 + slot // 8, owners, stride=held), :]
        piece = jnp.where((lane >> 4) == slot % 8, piece, 0.0).astype(bf16)
        table_ref[at, lanes:] = mm(piece, tile).astype(bf16)
    meta = rows_ref[pl.ds(19, owners, stride=held), :]
    blank = jnp.zeros((owners, lanes), f32)
    ropes = [blank] * (pages // 8)
    for start in range(pages - group, -1, -group):
        wanted = []
        for place in range(start + group - 1, start - 1, -1):
            owner = picks(meta[:, 32 + place : 33 + place] == lane.astype(f32))
            slot = jnp.broadcast_to(meta[:, 64 + place : 65 + place], (owners, lanes)).astype(bf16)
            one = jnp.concatenate(
                [jnp.where(slot == jnp.bfloat16(k), owner, jnp.bfloat16(0)) for k in range(slots)], axis=1
            )
            wanted.append(one if place > 0 else one[:16])
        found = mm(jnp.concatenate(wanted, axis=0), table_ref[...])
        for k in range(group):
            place = start + group - 1 - k
            if place > 0:
                got = found[k * owners : (k + 1) * owners]
            else:
                got = jnp.broadcast_to(found[k * owners : k * owners + 1], (owners, 2 * lanes))
            stage_ref[pl.ds(place, owners, stride=size), :] = got[:, :lanes]
            ropes[place // 8] += jnp.where((lane >> 4) == place % 8, got[:, lanes:], 0.0)
    comes = picks(meta[:, 96:97].astype(jnp.int32) == lane)
    arriving = mm_first(comes, rows_ref[pl.ds(16, owners, stride=held), :].astype(bf16))
    arriving_rope = mm_first(comes, jnp.where(lane < 16, meta, 0.0).astype(bf16))
    tail = [arriving] + ropes + [arriving_rope]
    tail += [blank] * (size - pages - len(tail))
    for k, piece in enumerate(tail):
        stage_ref[pl.ds(pages + k, owners, stride=size), :] = piece
    out_ref[...] = stage_ref[...].astype(bf16)


def collect(held, pages):
    owners = held.shape[0]
    held = held.reshape(owners * exchange_rows, lanes)
    out = pl.pallas_call(
        functools.partial(collect_kernel, pages, 4),
        in_specs=[pl.BlockSpec(memory_space=pltpu.VMEM)],
        out_specs=pl.BlockSpec(memory_space=pltpu.VMEM),
        out_shape=jax.ShapeDtypeStruct((owners * reply_rows, lanes), bf16),
        scratch_shapes=[
            pltpu.VMEM(held.shape, f32),
            pltpu.VMEM((owners * 16, 2 * lanes), bf16),
            pltpu.VMEM((owners * reply_rows, lanes), f32),
        ],
        compiler_params=pltpu.CompilerParams(vmem_limit_bytes=40 * 1024 * 1024),
        cost_estimate=pl.CostEstimate(flops=4 * 10**9, bytes_accessed=1_500_000, transcendentals=0),
    )(held)
    return out.reshape(owners, reply_rows // 2, 2, lanes)


factor = score_scale * log2_e


def joined(latent_ref, rope_ref, at):
    return jnp.concatenate([latent_ref[at, :], rope_ref[at, :]], axis=1)


def fresh_kernel(sub, q_ref, rope_ref, new_ref, acc_ref, stat_ref, value_ref, key_ref):
    latent = 4 * lanes

    @pl.when(pl.program_id(0) == 0)
    def build():
        fresh = new_ref[...].astype(f32)
        part = jnp.concatenate([fresh[:, :latent], jnp.zeros((64, latent), f32)], axis=0)
        value_ref[...] = part.astype(bf16)
        key_ref[:latent, :] = part.T.astype(bf16)
        rope = jnp.concatenate([fresh[:, latent:], jnp.zeros((64, 64), f32)], axis=0)
        key_ref[latent : latent + 64, :] = rope.T.astype(bf16)
        token = iota((64, lanes), 0)
        late = iota((64, lanes), 1)
        key_ref[latent + 64 :, :] = jnp.where(late <= token, 0.0, hidden).astype(bf16)

    for part in range(q_ref.shape[0] // sub):
        at = slice(part * sub, (part + 1) * sub)
        scores = mm(joined(q_ref, rope_ref, at), key_ref[...])
        top = jnp.max(scores, axis=1, keepdims=True)
        weight = jnp.exp2((scores - top) * jnp.float32(factor))
        total = jnp.sum(weight, axis=1, keepdims=True)
        acc_ref[at, :] = mm(weight.astype(bf16), value_ref[...])
        stat_ref[at, :] = jnp.where(iota((sub, lanes), 1) < 64, top, total)


def attend_fresh(queries, ropes, fresh, block=1024, sub=256):
    count, latent = queries.shape
    width = latent + lanes
    return pl.pallas_call(
        functools.partial(fresh_kernel, sub),
        grid=(count // block,),
        in_specs=[
            pl.BlockSpec((block, latent), lambda i: (i, 0)),
            pl.BlockSpec((block, lanes), lambda i: (i, 0)),
            pl.BlockSpec(fresh.shape, lambda i: (0, 0)),
        ],
        out_specs=[
            pl.BlockSpec((block, latent), lambda i: (i, 0)),
            pl.BlockSpec((block, lanes), lambda i: (i, 0)),
        ],
        out_shape=[
            jax.ShapeDtypeStruct((count, latent), f32),
            jax.ShapeDtypeStruct((count, lanes), f32),
        ],
        scratch_shapes=[pltpu.VMEM((lanes, latent), bf16), pltpu.VMEM((width, lanes), bf16)],
        compiler_params=pltpu.CompilerParams(vmem_limit_bytes=40 * 1024 * 1024),
        cost_estimate=pl.CostEstimate(flops=5 * 10**9, bytes_accessed=16_000_000, transcendentals=count * lanes),
    )(queries, ropes, fresh)


def unpack(pages, spot, length, ref, rows_ref, key_ref, arrive_ref):
    latent = 4 * lanes
    size = reply_rows
    rows = ref.shape[0] // (4 * size)
    half = rows * pages
    shift = rows.bit_length() - 1
    src = iota((lanes, lanes), 0)
    dst = iota((lanes, lanes), 1)
    lane = iota((rows, lanes), 1)
    rope_keys = jnp.zeros((half, lanes), f32)
    arrived_rope = jnp.zeros((rows, lanes), f32)
    rows_ref[...] = ref[...].astype(f32)
    for quarter in range(4):
        cols = slice(quarter * lanes, (quarter + 1) * lanes)
        take = lambda k: rows_ref[pl.ds(quarter * rows * size + k, rows, stride=size), :]
        for k in range(pages):
            key_ref[k * rows : (k + 1) * rows, cols] = take(k).astype(bf16)
        ropes = [take(pages + 1 + k) for k in range(pages // 8)]
        pieces = [jnp.where((lane >> 4) == k % 8, ropes[k // 8], 0.0) for k in range(pages)]
        rope = jnp.concatenate(pieces, axis=0).astype(bf16)
        put = picks(((dst >> 4) == quarter) & ((dst & 15) == (src & 15)))
        rope_keys += mm(rope, put)
        arrive_ref[:, cols] = take(pages)
        last = jnp.where(lane < 16, take(pages + 1 + pages // 8), 0.0)
        arrived_rope += mm(last.astype(bf16), put)
    arrive_ref[:, latent:] = arrived_rope[:, :64]
    key = iota((half, lanes), 0)
    place = (key >> shift) * 64 + (key & (rows - 1)) + spot
    bias = jnp.where(place < length, 0.0, hidden)
    extra = jnp.where(iota((half, lanes), 1) < 64, rope_keys, bias)
    key_ref[:, latent:] = extra.astype(bf16)


def unpack_kernel(pages, length_ref, own_ref, key_ref, arrive_ref, rows_ref):
    spot = lax.axis_index("pd") * (own_ref.shape[0] // (4 * reply_rows))
    unpack(pages, spot, length_ref[0], own_ref, rows_ref, key_ref, arrive_ref)


def unpack_own(length, own, pages, width):
    rows = own.shape[0] // (4 * reply_rows)
    inside = pl.BlockSpec(memory_space=pltpu.VMEM)
    return pl.pallas_call(
        functools.partial(unpack_kernel, pages),
        in_specs=[pl.BlockSpec(memory_space=pltpu.SMEM), inside],
        out_specs=[inside, inside],
        out_shape=[
            jax.ShapeDtypeStruct((rows * pages, 5 * lanes), bf16),
            jax.ShapeDtypeStruct((rows, width), f32),
        ],
        scratch_shapes=[pltpu.VMEM(own.shape, f32)],
        compiler_params=pltpu.CompilerParams(vmem_limit_bytes=40 * 1024 * 1024),
        cost_estimate=pl.CostEstimate(flops=10**9, bytes_accessed=2_000_000, transcendentals=0),
    )(length, own)


def attend_kernel(
    pages,
    sub,
    chunk,
    length_ref,
    dest_ref,
    q_ref,
    rope_ref,
    own_ref,
    mine_ref,
    peer_ref,
    acc_ref,
    stat_ref,
    cache_ref,
    out_ref,
    decode_ref,
    key_ref,
    score_ref,
    arrive_ref,
    rows_ref,
):
    latent = 4 * lanes
    rows = mine_ref.shape[0]
    half = rows * pages
    keys = 2 * half
    step = pl.program_id(0)

    def key_block(begin, cols):
        ref, at = (own_ref, begin) if begin < half else (key_ref, begin - half)
        return ref[at : at + chunk, cols]

    @pl.when(step == 0)
    def build():
        core = lax.axis_index("pd")
        spot = pl.multiple_of(core * rows, rows)
        other = pl.multiple_of((1 - core) * rows, rows)
        arrive_ref[pl.ds(spot, rows), :] = mine_ref[...]
        unpack(pages, other, length_ref[0], peer_ref, rows_ref, key_ref, arrive_ref.at[pl.ds(other, rows), :])

    count = q_ref.shape[0] // sub
    scale = jnp.float32(factor)

    def score(part):
        at = slice(part * sub, (part + 1) * sub)
        query = joined(q_ref, rope_ref, at)
        top = None
        for begin in range(0, keys, chunk):
            found = mm_last(query, key_block(begin, slice(None)))
            score_ref[part % 2, :, begin : begin + chunk] = found
            for k in range(0, chunk, lanes):
                piece = found[:, k : k + lanes]
                top = piece if top is None else jnp.maximum(top, piece)
        return jnp.maximum(jnp.max(top, axis=1, keepdims=True), stat_ref[at, :1])

    def finish(part, top):
        at = slice(part * sub, (part + 1) * sub)
        summed = None
        total = None
        for begin in range(0, keys, chunk):
            weight = jnp.exp2((score_ref[part % 2, :, begin : begin + chunk] - top) * scale)
            for k in range(0, chunk, lanes):
                piece = weight[:, k : k + lanes]
                total = piece if total is None else total + piece
            product = mm(weight.astype(bf16), key_block(begin, slice(0, latent)))
            summed = product if summed is None else summed + product
        shrink = jnp.exp2((stat_ref[at, :1] - top) * scale)
        total = jnp.sum(total, axis=1, keepdims=True) + shrink * stat_ref[at, 64:65]
        summed = summed + shrink * acc_ref[at, :]
        out_ref[at, :] = (summed * (1.0 / total)).astype(bf16)

    top = score(0)
    for part in range(count):
        after = score(part + 1) if part + 1 < count else None
        finish(part, top)
        top = after

    share = cache_ref.shape[0]
    for k in range(share):
        hit = dest_ref[0] == step * share + k
        decode_ref[k] = jnp.where(hit, arrive_ref[...], cache_ref[k].astype(f32)).astype(bf16)


def attend(length, dest, queries, ropes, own, mine, peer, acc, stat, cache, pages, block=1024, sub=256, chunk=256):
    count, latent = queries.shape
    width = latent + lanes
    keys = 64 * pages
    steps = count // block
    whole = lambda a: pl.BlockSpec(a.shape, lambda i: (0,) * a.ndim)
    strip = lambda w: pl.BlockSpec((block, w), lambda i: (i, 0))
    scalar = pl.BlockSpec(memory_space=pltpu.SMEM)
    share = pl.BlockSpec((cache.shape[0] // steps,) + cache.shape[1:], lambda i: (i, 0, 0))
    return pl.pallas_call(
        functools.partial(attend_kernel, pages, sub, chunk),
        grid=(steps,),
        in_specs=[scalar, scalar, strip(latent), strip(lanes), whole(own), whole(mine), whole(peer), strip(latent), strip(lanes), share],
        out_specs=[strip(latent), share],
        out_shape=[
            jax.ShapeDtypeStruct((count, latent), bf16),
            jax.ShapeDtypeStruct(cache.shape, bf16),
        ],
        scratch_shapes=[
            pltpu.VMEM((keys // 2, width), bf16),
            pltpu.VMEM((2, sub, keys), f32),
            pltpu.VMEM(cache.shape[1:], f32),
            pltpu.VMEM(peer.shape, f32),
        ],
        compiler_params=pltpu.CompilerParams(vmem_limit_bytes=48 * 1024 * 1024),
        cost_estimate=pl.CostEstimate(
            flops=2 * count * keys * (width + latent), bytes_accessed=20_000_000, transcendentals=count * keys
        ),
    )(length, dest, queries, ropes, own, mine, peer, acc, stat, cache)


def body(
    q_latent,
    q_rope,
    new_latent,
    pool_pages,
    page_owner,
    page_slot,
    prefix_len,
    partner,
    dest_slot,
    decode_cache,
):
    stretch, heads, latent = q_latent.shape
    rope = q_rope.shape[1] // heads

    outgoing = spread(partner, pool_pages, new_latent, page_owner, page_slot)
    held = lax.all_to_all(outgoing, "pool", split_axis=0, concat_axis=0, tiled=True)

    token = jnp.arange(stretch, dtype=jnp.int32)
    mark = jnp.broadcast_to(
        (token[:, None] == token[None, :]).astype(bf16)[:, None, :], (stretch, heads, stretch)
    )
    ropes = jnp.concatenate([q_rope.reshape(stretch, heads, rope), mark], axis=2)
    ropes = ropes.reshape(stretch * heads, lanes)
    queries = q_latent.reshape(stretch * heads, latent)
    acc, stat = attend_fresh(queries, ropes, new_latent)
    held, acc, stat = lax.optimization_barrier((held, acc, stat))

    pages = page_owner.shape[1]
    own = lax.all_to_all(collect(held, pages), "pool", split_axis=0, concat_axis=0, tiled=True)
    own = own.reshape(-1, lanes)
    peer = lax.ppermute(own, "pd", [(0, 1), (1, 0)])
    own, mine = unpack_own(prefix_len, own, pages, new_latent.shape[1])
    context, decode_out = attend(prefix_len, dest_slot, queries, ropes, own, mine, peer, acc, stat, decode_cache, pages)
    return (context.reshape(stretch, heads, latent), decode_out)


def solution(mesh):
    placed = (
        P("pool", "pd", None),
        P("pool", "pd"),
        P("pool", None),
        P("pool", None, None),
        P("pool", None),
        P("pool", None),
        P("pool"),
        P("pool"),
        P("pool"),
        P("pool", None, None),
    )
    return jax.shard_map(
        body,
        mesh=mesh,
        in_specs=placed,
        out_specs=(P("pool", "pd", None), P("pool", None, None)),
        check_vma=False,
    )
```
